128 devices in a mesh: tau: 16 (over z, x_lo, core), aux: 8 (over x_hi, y).
Axes of the slice: x: 4 (x_hi: 2, x_lo: 2; x = x_hi * 2 + x_lo), y: 4, z: 4, core: 2. Of those that a mesh axis runs over, the one named last changes fastest.
Arguments:
- green_tau: bfloat16 [128, 256, 20480], P('tau', None, 'aux'), may hold values from -6 to 6
- fit_matrix: bfloat16 [72, 128], replicated, may hold values from -0.5 to 0.5
- aux_factors: bfloat16 [2048, 20480], P(None, 'aux'), may hold values from -0.0625 to 0.0625
- freq_basis: float32 [240, 72], replicated, may hold values from -0.75 to 0.75
- screened: float32 [120, 2048], P(None, 'aux'), may hold values from 0.5 to 2
- pair_mask: int32 [256, 160], P('tau', 'aux'), may hold values 0 or 1
Outputs:
- sigma: float32 [240, 256, 2048], P(None, 'tau', 'aux')
The draws below stay inside these ranges and needn't reach their ends.
All inputs are finite; a program needn't handle non-finite values. No bound on the sum of `pair_mask` on one device may be relied on, other than what follows from the above.
Results may differ from the reference program's by a relative error of at most 0.0029.
Values may be sent and summed in bfloat16 or wider, within the bound.
No kernel may reach another device: no remote copies, remote signals or barrier semaphores. Data moves between devices by JAX's collectives and lax.ppermute only.
A program may use at most 128 MiB of HBM per device.

```python
import math
import jax
import jax.numpy as jnp
from jax import lax

NTAU = 128
ROWS = 256
B = 20480
BLOCK = 128
NBLK = 160
NL = 72
NW = 120
NAUX = 2048


def plant(drawn, key, smallest, largest):
    extent = drawn.shape
    index_at = [jax.random.randint(jax.random.fold_in(key, axis), (), 0, extent[axis]) for axis in range(len(extent))]
    drawn = drawn.at[tuple(index_at)].set(smallest)
    longest = extent.index(max(extent))
    index_at[longest] = (index_at[longest] + 1) % extent[longest]
    return drawn.at[tuple(index_at)].set(largest)


def with_spikes(result, own_key, source, target, shards_of, factor):
    def block_of(axis_at):
        return (jnp.arange(result.shape[axis_at]) // (result.shape[axis_at] // shards_of)).reshape((-1,) + (1,) * (result.ndim - 1 - axis_at))

    near = jax.random.permutation(own_key, shards_of)[block_of(target)]
    second = (block_of(target) + shards_of // 2) % shards_of
    return jnp.where((block_of(source) == near) | (block_of(source) == second), factor * result, result)


def steps_of(stream_key, extent, split, low, top_value):
    loudness = 1.0
    for dim, shards_of in split:
        draws = jax.random.uniform(jax.random.fold_in(jax.random.fold_in(stream_key, 6), dim), (shards_of,), jnp.float32, low / len(split), top_value / len(split))
        loudness = loudness * jnp.repeat(jnp.exp(draws), extent[dim] // shards_of).reshape((-1,) + (1,) * (len(extent) - 1 - dim))
    return loudness


def gaussian(own_key, extent, deviation, bound, cuts=(), held_as=jnp.bfloat16):
    loudness = steps_of(own_key, extent, cuts, -0.22, 0.18) if cuts else 1.0
    values = jax.random.normal(own_key, extent, jnp.float32) * deviation * loudness
    return jnp.minimum(jnp.maximum(values, -bound), bound).astype(held_as)


def noise_with(own_key, shape, deviation, most, cuts, heavy, dtype=jnp.bfloat16):
    entries = deviation * jax.random.normal(own_key, shape, jnp.float32)
    if cuts:
        entries = entries * steps_of(own_key, shape, cuts, -0.22, 0.18)
    return jnp.clip(with_spikes(entries, jax.random.fold_in(own_key, 3), *heavy), -most, most).astype(dtype)


def setup_inputs(seed: int = 0) -> dict:
    arg_keys = jax.random.split(jax.random.key(seed), 7)
    green_tau = gaussian(arg_keys[0], (NTAU, ROWS, B), 1.0, 6.0, ((0, 16), (2, 8)))
    fit_matrix = gaussian(arg_keys[1], (NL, NTAU), NTAU ** -0.5, 0.5)
    aux_factors = noise_with(arg_keys[2], (NAUX, B), B ** -0.5, 0.0625, ((1, 8),), (1, 0, 8, 2.0))
    freq_basis = gaussian(arg_keys[3], (2 * NW, NL), NL ** -0.5, 0.75, (), jnp.float32)
    screened = jnp.clip(jnp.exp(math.log(2.0) - 1.3862944 * jax.random.uniform(arg_keys[4], (NW, NAUX), jnp.float32) ** steps_of(arg_keys[4], (NW, NAUX), ((1, 8),), -0.2, 0.2)), 0.5, 2.0)
    pair_mask = plant((jax.random.randint(arg_keys[5], (ROWS, NBLK), 0, 2) < 1).astype(jnp.int32), jax.random.fold_in(arg_keys[5], 1), 0, 1)
    return dict(green_tau=green_tau, fit_matrix=fit_matrix, aux_factors=aux_factors, freq_basis=freq_basis, screened=screened, pair_mask=pair_mask)


def reference(green_tau, fit_matrix, aux_factors, freq_basis, screened, pair_mask):
    fit_wide = fit_matrix.astype(jnp.float32)
    aux_wide = aux_factors.astype(jnp.float32)

    def one_row(pieces):
        row_times, marks = pieces
        coeff = jnp.dot(fit_wide, row_times.astype(jnp.float32), precision=lax.Precision.HIGHEST)
        keeper = jnp.repeat(marks.astype(jnp.float32), BLOCK)
        rounded = lax.optimization_barrier((coeff * keeper[None, :]).astype(jnp.bfloat16))
        return jnp.dot(rounded.astype(jnp.float32), aux_wide.T, precision=lax.Precision.HIGHEST)

    proj = lax.map(one_row, (jnp.moveaxis(green_tau, 1, 0), pair_mask))
    mixed = jnp.einsum("wl,mlp->wmp", freq_basis, proj, precision=lax.Precision.HIGHEST)
    weight = jnp.concatenate([screened, screened], axis=0)
    return mixed * weight[:, None, :]
```

```python
import functools

import jax
import jax.numpy as jnp
import numpy as np
from jax import lax
from jax.experimental import pallas as pl
from jax.experimental.pallas import tpu as pltpu
from jax.sharding import Mesh, PartitionSpec as P

BLOCK = 128
ORDER = (2, 1, 3, 0)


def fill(g_refs, mask_ref, rows_ref):
    times, _, height, cols = g_refs[0].shape
    blocks = mask_ref.shape[-1]
    lane = lax.broadcasted_iota(jnp.int32, (blocks, cols), 1)
    first = lax.broadcasted_iota(jnp.int32, (blocks, cols), 0) * BLOCK
    spread = jnp.where((lane >= first) & (lane < first + BLOCK), 1.0, 0.0).astype(jnp.bfloat16)
    for i, g_ref in enumerate(g_refs):
        marks = mask_ref[i].astype(jnp.float32).astype(jnp.bfloat16)
        keep = jnp.dot(marks, spread, preferred_element_type=jnp.float32).astype(jnp.bfloat16)
        for t in range(times):
            at = (i * times + t) * height
            rows_ref[at : at + height] = g_ref[t, 0] * keep


def product(rows_ref, a_ref):
    return lax.dot_general(
        rows_ref[...], a_ref[0, 0], (((1,), (1,)), ((), ())), preferred_element_type=jnp.float32
    )


def far_kernel(at, mask_ref, g0, g1, g2, g3, a_ref, lo_ref, hi_ref, rows_ref):
    j = pl.program_id(0)

    @pl.when(j == 0)
    def _():
        fill((g0, g1, g2, g3), mask_ref, rows_ref)
        lo_ref[...] = product(rows_ref, a_ref).astype(jnp.bfloat16)

    @pl.when(j == 1)
    def _():
        hi_ref[...] = product(rows_ref, a_ref).astype(jnp.bfloat16)


def near_kernel(at, mask_ref, g0, g1, g2, g3, a_ref, from_up, from_down, down_ref, up_ref, rows_ref):
    j = pl.program_id(0)

    @pl.when(j == 0)
    def _():
        fill((g0, g1, g2, g3), mask_ref, rows_ref)
        down_ref[0] = (product(rows_ref, a_ref) + from_up[...].astype(jnp.float32)).astype(jnp.bfloat16)

    @pl.when(j == 1)
    def _():
        down_ref[0] = product(rows_ref, a_ref).astype(jnp.bfloat16)

    @pl.when(j == 2)
    def _():
        up_ref[0] = product(rows_ref, a_ref).astype(jnp.bfloat16)

    @pl.when(j == 3)
    def _():
        up_ref[0] = (product(rows_ref, a_ref) + from_down[...].astype(jnp.float32)).astype(jnp.bfloat16)


def own_kernel(at, mask_ref, g0, g1, g2, g3, a_ref, from_up, from_down, own_ref, other_ref, rows_ref):
    j = pl.program_id(0)

    def total():
        return product(rows_ref, a_ref) + (from_up[0].astype(jnp.float32) + from_down[0].astype(jnp.float32))

    @pl.when(j == 0)
    def _():
        fill((g0, g1, g2, g3), mask_ref, rows_ref)
        other_ref[...] = total()

    @pl.when(j == 1)
    def _():
        own_ref[...] = total()


def call(kernel, steps, aux_at, at, chunk, marks, green, aux, extra, extra_specs, out_shape, out_specs):
    times, _, height, cols = green.shape
    width = aux.shape[2]

    def owner(i):
        return lambda j, at: (0, at[2 + chunk * 4 + i], 0, 0)

    return pl.pallas_call(
        kernel,
        grid_spec=pltpu.PrefetchScalarGridSpec(
            num_scalar_prefetch=1,
            grid=(steps,),
            in_specs=[pl.BlockSpec(marks.shape, lambda j, at: (0, 0, 0))]
            + [pl.BlockSpec((times, 1, height, cols), owner(i)) for i in range(4)]
            + [pl.BlockSpec((1, 1, width, cols), lambda j, at: (*aux_at(j, at), 0, 0))]
            + extra_specs,
            out_specs=out_specs,
            scratch_shapes=[pltpu.VMEM((4 * times * height, cols), jnp.bfloat16)],
        ),
        out_shape=out_shape,
        compiler_params=pltpu.CompilerParams(vmem_limit_bytes=40 * 2**20),
        cost_estimate=pl.CostEstimate(
            flops=2 * steps * 4 * times * height * cols * width,
            bytes_accessed=2 * cols * (4 * times * height + steps * width),
            transcendentals=0,
        ),
    )(at, marks, green, green, green, green, aux, *extra)


def body(green_tau, fit_matrix, aux_factors, freq_basis, screened, pair_mask):
    z, xl, c, xh, y = (lax.axis_index(a) for a in ("z", "xl", "c", "xh", "y"))
    nz, ny = lax.axis_size("z"), lax.axis_size("y")
    times, n_rows, cols = green_tau.shape
    height = pair_mask.shape[0]
    green = green_tau.reshape(times, n_rows // height, height, cols)
    width = aux_factors.shape[0] // (2 * ny)
    aux = aux_factors.reshape(2, ny, width, cols)
    rows = 4 * times * height

    def shift(v, axis, by):
        n = lax.axis_size(axis)
        return lax.ppermute(v, axis, [(i, (i + by) % n) for i in range(n)])

    def flip(v, axis):
        return lax.ppermute(v, axis, [(0, 1), (1, 0)])

    pair = jnp.stack([pair_mask, flip(pair_mask, "c")])
    quad = jnp.concatenate([pair, flip(pair, "xl")])
    marks = [quad if d == 0 else shift(quad, "z", -d) for d in range(nz)]

    owners = [((z + d) % nz) * 4 + (xl ^ e) * 2 + (c ^ f) for d in range(nz) for e in (0, 1) for f in (0, 1)]
    at = jnp.stack([xh, y] + owners).astype(jnp.int32)

    half = jax.ShapeDtypeStruct((rows, width), jnp.bfloat16)
    whole = jax.ShapeDtypeStruct((2, rows, width), jnp.bfloat16)
    total = jax.ShapeDtypeStruct((rows, width), jnp.float32)
    fixed = pl.BlockSpec((rows, width), lambda j, at: (0, 0))

    arrived = [None] * nz
    step1 = {}
    for d in ORDER:
        lo, hi = call(
            far_kernel, 2, lambda j, at: (j, (at[1] + 2) % ny), at, d, marks[d], green, aux,
            [], [], [half, half], [fixed, fixed],
        )
        step1[d] = shift(lo, "y", -1), shift(hi, "y", 1)
    for d in ORDER:
        down, up = call(
            near_kernel, 4, lambda j, at: (j % 2, (at[1] + ny - 1 + 2 * (j // 2)) % ny), at, d, marks[d], green, aux,
            list(step1[d]), [fixed, fixed], [whole, whole],
            [
                pl.BlockSpec((1, rows, width), lambda j, at: (jnp.minimum(j, 1), 0, 0)),
                pl.BlockSpec((1, rows, width), lambda j, at: (jnp.maximum(j - 2, 0), 0, 0)),
            ],
        )
        from_up, from_down = shift(down, "y", -1), shift(up, "y", 1)
        mine = pl.BlockSpec((1, rows, width), lambda j, at: (at[0] ^ (1 - j), 0, 0))
        own, other = call(
            own_kernel, 2, lambda j, at: (at[0] ^ (1 - j), at[1]), at, d, marks[d], green, aux,
            [from_up, from_down], [mine, mine], [total, total], [fixed, fixed],
        )
        summed = own + flip(other, "xh")
        kept, sent = summed[: rows // 2], summed[rows // 2 :]
        both = jnp.stack([kept, flip(sent, "xl")]).reshape(2, 2, times, height, width)
        arrived[d] = both if d == 0 else shift(both, "z", d)
    held = jnp.stack(arrived)
    sent = flip(held[:, :, 1], "c")
    x = jnp.stack([held[:, :, 0], sent], axis=2).reshape(nz * 4 * times, height, width)

    order = [((z + nz - d) % nz) * 4 + (xl ^ e) * 2 + (c ^ f) for d in range(nz) for e in (0, 1) for f in (0, 1)]
    source = jnp.stack(order)[:, None] * times + jnp.arange(times)[None, :]
    pick = (jnp.arange(nz * 4 * times)[:, None] == source.reshape(1, -1)).astype(jnp.float32)
    exact = lax.Precision.HIGHEST
    picked = jnp.dot(fit_matrix.astype(jnp.float32), pick, precision=exact)
    weights = jnp.dot(freq_basis, picked, precision=exact)
    mixed = jnp.einsum("wt,tmp->wmp", weights, x, precision=exact)
    return mixed * jnp.concatenate([screened, screened], axis=0)[:, None, :]


def solution(mesh):
    devices = np.array(mesh.devices).reshape(4, 2, 2, 2, 4)
    fine = Mesh(devices, ("z", "xl", "c", "xh", "y"))
    tau, aux = ("z", "xl", "c"), ("xh", "y")
    return jax.shard_map(
        body,
        mesh=fine,
        in_specs=(P(tau, None, aux), P(), P(None, aux), P(), P(None, aux), P(tau, aux)),
        out_specs=P(None, tau, aux),
        check_vma=False,
    )
```

```python
import jax
import jax.numpy as jnp
import numpy as np
from jax import lax
from jax.experimental import pallas as pl
from jax.experimental.pallas import tpu as pltpu
from jax.sharding import Mesh, PartitionSpec as P

BLOCK = 128
LANES = 128
AWAY = (2, 1, 3)
PARAMS = pltpu.CompilerParams(vmem_limit_bytes=56 * 2**20)
ANY = pl.BlockSpec(memory_space=pl.ANY)


def fill(g_refs, mask_ref, picks, rows_ref):
    times, _, height, cols = g_refs[0].shape
    for i, g_ref in enumerate(g_refs):
        marks = mask_ref[picks[i]].astype(jnp.float32)
        for k in range(cols // BLOCK):
            keep = jnp.broadcast_to(marks[:, k : k + 1], (height, BLOCK)).astype(jnp.bfloat16)
            at = slice(k * BLOCK, (k + 1) * BLOCK)
            for t in range(times):
                row = (i * times + t) * height
                rows_ref[row : row + height, at] = g_ref[t, 0, :, at] * keep


def product(rows_ref, a):
    return lax.dot_general(rows_ref[...], a, (((1,), (1,)), ((), ())), preferred_element_type=jnp.float32)


def cross_kernel(at, mask_ref, g0, g1, g2, g3, a_ref, b_ref, l_ref, h_ref, o_ref, rows_ref):
    j = pl.program_id(0)

    @pl.when(j == 0)
    def _():
        c = at[2]
        fill((g0, g1, g2, g3), mask_ref, (c, 1 - c, 2 + c, 3 - c), rows_ref)

    part = rows_ref.shape[0] // 4
    width = o_ref.shape[3]

    def put(near_ref, far_ref):
        v = product(rows_ref, a_ref[0])
        for k in range(2):
            for f in range(2):
                at_col = slice(k * width, (k + 1) * width)
                near_ref[f, k] = v[f * part : (f + 1) * part, at_col].astype(near_ref.dtype)
                far_ref[f, k] = v[(2 + f) * part : (3 + f) * part, at_col].astype(far_ref.dtype)

    @pl.when(j < 2)
    def _():
        put(h_ref, b_ref)

    @pl.when(j >= 2)
    def _():
        put(o_ref, l_ref)


def far_kernel(at, mask_ref, g0, g1, g2, g3, a0, a1, after, lo_ref, hi_ref, rows_ref):
    fill((g0, g1, g2, g3), mask_ref, range(4), rows_ref)
    lo_ref[...] = product(rows_ref, a0[0, 0]).astype(jnp.bfloat16)
    hi_ref[...] = product(rows_ref, a1[0, 0]).astype(jnp.bfloat16)


def near_kernel(at, mask_ref, g0, g1, g2, g3, a0, a1, from_up, from_down, after, down_ref, up_ref, rows_ref):
    s = pl.program_id(1)

    @pl.when(s == 0)
    def _():
        fill((g0, g1, g2, g3), mask_ref, range(4), rows_ref)
        down_ref[0, 0] = (product(rows_ref, a0[0, 0]) + from_up[...].astype(jnp.float32)).astype(jnp.bfloat16)
        down_ref[0, 1] = product(rows_ref, a1[0, 0]).astype(jnp.bfloat16)

    @pl.when(s == 1)
    def _():
        up_ref[0, 0] = product(rows_ref, a0[0, 0]).astype(jnp.bfloat16)
        up_ref[0, 1] = (product(rows_ref, a1[0, 0]) + from_down[...].astype(jnp.float32)).astype(jnp.bfloat16)


def own_kernel(at, mask_ref, g0, g1, g2, g3, a0, a1, after, own_ref, rows_ref):
    fill((g0, g1, g2, g3), mask_ref, range(4), rows_ref)
    own_ref[0, 0] = product(rows_ref, a0[0, 0])
    own_ref[0, 1] = product(rows_ref, a1[0, 0])


def final_kernel(w_ref, s_ref, x0_ref, xk_ref, xr_ref, o_ref):
    n_freq, n_time = w_ref.shape
    height = o_ref.shape[0] // n_freq
    part = 8 * height
    w = w_ref[...]
    high = w.astype(jnp.bfloat16)
    low = (w - high.astype(jnp.float32)).astype(jnp.bfloat16)
    twice = jnp.concatenate([high, high], axis=1)
    scale = jnp.concatenate([s_ref[...], s_ref[...]], axis=0)

    def row(m):
        return jnp.concatenate(
            [
                ref[pl.ds(i * part + m, 8, stride=height), :]
                for ref in (x0_ref, xk_ref, xr_ref)
                for i in range(ref.shape[0] // part)
            ],
            axis=0,
        )

    for m in range(0, height, 2):
        x = jnp.concatenate([row(m), row(m + 1)], axis=1)
        x_high = x.astype(jnp.bfloat16)
        x_low = (x - x_high.astype(jnp.float32)).astype(jnp.bfloat16)
        mixed = jnp.dot(
            twice, jnp.concatenate([x_high, x_low], axis=0), preferred_element_type=jnp.float32
        ) + jnp.dot(low, x_high, preferred_element_type=jnp.float32)
        o_ref[pl.ds(m, n_freq, stride=height), :] = mixed[:, :LANES] * scale
        o_ref[pl.ds(m + 1, n_freq, stride=height), :] = mixed[:, LANES:] * scale


def body(green_tau, fit_matrix, aux_factors, freq_basis, screened, pair_mask):
    z, xl, c, xh, y = (lax.axis_index(a) for a in ("z", "xl", "c", "xh", "y"))
    nz, ny = lax.axis_size("z"), lax.axis_size("y")
    times, n_rows, cols = green_tau.shape
    height = pair_mask.shape[0]
    green = green_tau.reshape(times, n_rows // height, height, cols)
    n_aux = aux_factors.shape[0]
    width = n_aux // (2 * ny)
    aux = aux_factors.reshape(2, ny, width, cols)
    part = times * height
    rows = 4 * part
    f32, bf16 = jnp.float32, jnp.bfloat16

    def shift(v, axis, by):
        n = lax.axis_size(axis)
        return lax.ppermute(v, axis, [(i, (i + by) % n) for i in range(n)])

    def flip(v, axis):
        return lax.ppermute(v, axis, [(0, 1), (1, 0)])

    def send(v, d, e, h):
        pairs = [
            (i * 4 + j * 2 + k, (i + d) % nz * 4 + (j ^ e) * 2 + (k ^ h))
            for i in range(nz) for j in (0, 1) for k in (0, 1)
        ]
        return lax.ppermute(v, ("z", "xl", "xh"), pairs)

    pair = jnp.stack([pair_mask, flip(pair_mask, "c")])
    quad = jnp.concatenate([pair, flip(pair, "xl")])
    away = [shift(quad, "z", -d) for d in AWAY]

    owners = [z * 4 + (xl ^ e) * 2 + f for e in (0, 1) for f in (0, 1)]
    owners += [(z + d) % nz * 4 + (xl ^ e) * 2 + (c ^ f) for d in AWAY for e in (0, 1) for f in (0, 1)]
    at = jnp.stack([xh, y, c] + owners).astype(jnp.int32)

    def inputs(first, marks):
        def chunk(g):
            return first + g[0] if first else 0

        def owner(i):
            return lambda *g: (0, g[-1][3 + chunk(g) * 4 + i], 0, 0)

        return [pl.BlockSpec((4, *marks.shape[1:]), lambda *g: (g[0] if first else 0, 0, 0))] + [
            pl.BlockSpec((times, 1, height, cols), owner(i)) for i in range(4)
        ]

    def aux_at(h, target):
        return pl.BlockSpec((1, 1, width, cols), lambda *g: (g[-1][0] ^ h, target(*g), 0, 0))

    def call(kernel, grid, in_specs, out_specs, out_shape, args, columns):
        return pl.pallas_call(
            kernel,
            grid_spec=pltpu.PrefetchScalarGridSpec(
                num_scalar_prefetch=1,
                grid=grid,
                in_specs=in_specs,
                out_specs=out_specs,
                scratch_shapes=[pltpu.VMEM((rows, cols), bf16)],
            ),
            out_shape=out_shape,
            compiler_params=PARAMS,
            cost_estimate=pl.CostEstimate(
                flops=2 * rows * cols * columns, bytes_accessed=2 * cols * (rows + columns), transcendentals=0
            ),
        )(at, *args)

    def many(n):
        return jax.ShapeDtypeStruct((2, ny, part, width), n)

    first = pl.BlockSpec((2, 2, part, width), lambda j, at: (0, jnp.minimum(j, 1), 0, 0))
    second = pl.BlockSpec((2, 2, part, width), lambda j, at: (0, jnp.maximum(j - 2, 0), 0, 0))
    to_both, to_low, to_high, kept = call(
        cross_kernel, (4,),
        inputs(0, quad)
        + [pl.BlockSpec((1, n_aux // 4, cols), lambda j, at: (at[0] ^ (1 - j // 2), j % 2, 0))],
        [first, second, first, second],
        [many(bf16), many(bf16), many(bf16), many(f32)],
        (quad, green, green, green, green, aux_factors.reshape(2, n_aux // 2, cols)), n_aux,
    )
    got_both, got_low, got_high = send(to_both, 0, 1, 1), send(to_low, 0, 1, 0), send(to_high, 0, 0, 1)

    def far(i, n, after):
        marks = jnp.concatenate(away[i : i + n])
        two = lambda q, at: (at[1] + 2) % ny
        out = pl.BlockSpec((rows, width), lambda q, at: (q, 0))
        shape = jax.ShapeDtypeStruct((n * rows, width), bf16)
        lo, hi = call(
            far_kernel, (n,), inputs(1 + i, marks) + [aux_at(0, two), aux_at(1, two), ANY],
            [out, out], [shape, shape], (marks, *[green] * 4, aux, aux, after), 2 * width * n,
        )
        return lo, shift(lo, "y", -1), shift(hi, "y", 1)

    def near(i, n, lo, hi, after):
        marks = jnp.concatenate(away[i : i + n])
        side = lambda q, s, at: (at[1] + ny - 1 + 2 * s) % ny
        got = pl.BlockSpec((rows, width), lambda q, s, at: (q, 0))
        out = pl.BlockSpec((1, 2, rows, width), lambda q, s, at: (q, 0, 0, 0))
        shape = jax.ShapeDtypeStruct((n, 2, rows, width), bf16)
        down, up = call(
            near_kernel, (n, 2), inputs(1 + i, marks) + [aux_at(0, side), aux_at(1, side), got, got, ANY],
            [out, out], [shape, shape], (marks, *[green] * 4, aux, aux, lo, hi, after), 4 * width * n,
        )
        return down, shift(down, "y", -1), shift(up, "y", 1)

    lo_a, up_a, down_a = far(0, 1, kept)
    lo_b, up_b, down_b = far(1, 2, lo_a)
    near_a, from_up_a, from_down_a = near(0, 1, up_a, down_a, lo_b)
    near_b, from_up_b, from_down_b = near(1, 2, up_b, down_b, near_a)
    marks = jnp.concatenate(away)
    here = lambda q, at: at[1]
    own = call(
        own_kernel, (3,), inputs(1, marks) + [aux_at(0, here), aux_at(1, here), ANY],
        pl.BlockSpec((1, 2, rows, width), lambda q, at: (q, 0, 0, 0)),
        jax.ShapeDtypeStruct((3, 2, rows, width), f32), (marks, *[green] * 4, aux, aux, near_b), 6 * width,
    )

    def deliver(d, total):
        quarter = total.reshape(2, 2, 2 * part, width)
        r00 = send(quarter[0, 0], d, 0, 0)
        r01 = send(quarter[0, 1].astype(bf16), d, 1, 0)
        r10 = send(quarter[1, 0].astype(bf16), d, 0, 1)
        r11 = send(quarter[1, 1].astype(bf16), d, 1, 1)
        return r00 + r10.astype(f32), r01.astype(f32) + r11.astype(f32)

    pieces = []
    for k, d in enumerate(AWAY):
        up, down = (from_up_a[0], from_down_a[0]) if k == 0 else (from_up_b[k - 1], from_down_b[k - 1])
        pieces += deliver(d, own[k] + (up.astype(f32) + down.astype(f32)))
    x_kept = jnp.concatenate([v[:part] for v in pieces])
    x_got = flip(jnp.concatenate([v[part:] for v in pieces]), "c")

    zero = kept + got_high.astype(f32)
    one = got_both.astype(f32) + got_low.astype(f32)
    crossing = jnp.stack([zero, one], axis=2).astype(bf16).reshape(2 * ny, 2, part, width)
    crossing, _ = lax.optimization_barrier((crossing, from_up_b))
    crossed = lax.all_to_all(crossing, ("c", "y"), split_axis=0, concat_axis=0, tiled=True)
    x_home = crossed.reshape(2, ny, 2, part, width).astype(f32).sum(axis=1).reshape(4 * part, width)

    order = [z * 4 + (xl ^ e) * 2 + f for f in (0, 1) for e in (0, 1)]
    for side in (c, 1 - c):
        order += [(z + nz - d) % nz * 4 + (xl ^ e) * 2 + side for d in AWAY for e in (0, 1)]
    source = (jnp.stack(order)[:, None] * times + jnp.arange(times)[None, :]).reshape(1, -1)
    n_time = source.shape[1]
    pick = (jnp.arange(n_time)[:, None] == source).astype(f32)
    exact = lax.Precision.HIGHEST
    picked = jnp.dot(fit_matrix.astype(f32), pick, precision=exact)
    weights = jnp.dot(freq_basis, picked, precision=exact)

    n_freq = weights.shape[0]
    lane = lambda v: pl.BlockSpec((v.shape[0], LANES), lambda j: (0, j))
    sigma = pl.pallas_call(
        final_kernel,
        grid=(width // LANES,),
        in_specs=[pl.BlockSpec(weights.shape, lambda j: (0, 0))] + [lane(v) for v in (screened, x_home, x_kept, x_got)],
        out_specs=pl.BlockSpec((n_freq * height, LANES), lambda j: (0, j)),
        out_shape=jax.ShapeDtypeStruct((n_freq * height, width), f32),
        compiler_params=PARAMS,
    )(weights, screened, x_home, x_kept, x_got)
    return sigma.reshape(n_freq, height, width)


def solution(mesh):
    devices = np.array(mesh.devices).reshape(4, 2, 2, 2, 4)
    fine = Mesh(devices, ("z", "xl", "c", "xh", "y"))
    tau, aux = ("z", "xl", "c"), ("xh", "y")
    return jax.shard_map(
        body,
        mesh=fine,
        in_specs=(P(tau, None, aux), P(), P(None, aux), P(), P(None, aux), P(tau, aux)),
        out_specs=P(None, tau, aux),
        check_vma=False,
    )
```

```python
import functools

import jax
import jax.numpy as jnp
import numpy as np
from jax import lax
from jax.experimental import pallas as pl
from jax.experimental.pallas import tpu as pltpu
from jax.sharding import Mesh, PartitionSpec as P

BLOCK = 128
LANES = 128
ANY = pl.BlockSpec(memory_space=pl.ANY)
WHOLE = pl.BlockSpec(memory_space=pltpu.VMEM)
SMALL = pltpu.CompilerParams(vmem_limit_bytes=14 * 2**20)
COST = pl.CostEstimate(flops=4 * 10**9, bytes_accessed=2 * 10**7, transcendentals=0)
LITTLE = pl.CostEstimate(flops=10**6, bytes_accessed=10**5, transcendentals=0)
LONG = pl.CostEstimate(flops=10**11, bytes_accessed=10**6, transcendentals=0)


def stage_kernel(source, after, held, sem):
    copy = pltpu.make_async_copy(source, held, sem)
    copy.start()
    copy.wait()


def join_kernel(a, b, c, d, out):
    for i, v in enumerate((a, b, c, d)):
        out[i] = v[...]


def fill(at, chunk, green_ref, mask_ref, rows_ref):
    times, _, height, cols = green_ref.shape
    base = lax.rem(at[2] + chunk, 4) * 4
    for i in range(4):
        marks = mask_ref[i ^ at[1]].astype(jnp.float32)
        for k in range(cols // BLOCK):
            keep = jnp.broadcast_to(marks[:, k : k + 1], (height, BLOCK)).astype(jnp.bfloat16)
            lanes = slice(k * BLOCK, (k + 1) * BLOCK)
            for t in range(times):
                row = (i * times + t) * height
                rows_ref[row : row + height, lanes] = green_ref[t, base + i, :, lanes] * keep


def product(rows_ref, a):
    return lax.dot_general(rows_ref[...], a, (((1,), (1,)), ((), ())), preferred_element_type=jnp.float32)


def put(out_ref, h, v):
    part = out_ref.shape[2]
    for i in range(4):
        out_ref[i, h] = v[i * part : (i + 1) * part].astype(out_ref.dtype)


def far_kernel(chunks, at, green_ref, aux_ref, after, *refs):
    mask_refs, (lo_ref, hi_ref, rows_ref) = refs[: len(chunks)], refs[len(chunks) :]
    target = lax.rem(at[0] + 2, aux_ref.shape[1])
    for q, chunk in enumerate(chunks):
        fill(at, chunk, green_ref, mask_refs[q], rows_ref)
        lo_ref[q] = product(rows_ref, aux_ref[0, target]).astype(jnp.bfloat16)
        hi_ref[q] = product(rows_ref, aux_ref[1, target]).astype(jnp.bfloat16)


def near_kernel(chunk, at, green_ref, aux_ref, after, mask_ref, from_up, from_down, *refs):
    down_ref, up_ref, rows_ref = refs[-3:]
    n = aux_ref.shape[1]
    fill(at, chunk, green_ref, mask_ref, rows_ref)
    below, above = lax.rem(at[0] + n - 1, n), lax.rem(at[0] + 1, n)
    put(down_ref, 0, product(rows_ref, aux_ref[0, below]) + from_up[0].astype(jnp.float32))
    put(down_ref, 1, product(rows_ref, aux_ref[1, below]))
    put(up_ref, 0, product(rows_ref, aux_ref[0, above]))
    put(up_ref, 1, product(rows_ref, aux_ref[1, above]) + from_down[0].astype(jnp.float32))


def own_kernel(at, green_ref, aux_ref, after, mask_refs, out_ref, rows_ref):
    chunk = pl.program_id(0)
    fill(at, chunk, green_ref, mask_refs, rows_ref)
    for h in range(2):
        put(out_ref.at[0], h, product(rows_ref, aux_ref[h, at[0]]))


def sum_kernel(own_ref, from_up, from_down, after, out_ref):
    for i in range(4):
        for h in range(2):
            others = from_up[i, h].astype(jnp.float32) + from_down[i, h].astype(jnp.float32)
            out_ref[i, h] = (own_ref[0, i, h] + others).astype(out_ref.dtype)


def gather_kernel(got_ref, after, out_ref):
    part = got_ref.shape[1]
    for i in range(got_ref.shape[0] // 2):
        both = got_ref[2 * i].astype(jnp.float32) + got_ref[2 * i + 1].astype(jnp.float32)
        out_ref[i * part : (i + 1) * part] = both


def final_kernel(w_ref, s_ref, *refs):
    x_refs, o_ref = refs[:-1], refs[-1]
    n_freq, _ = w_ref.shape
    height = o_ref.shape[0] // n_freq
    part = 8 * height
    w = w_ref[...]
    high = w.astype(jnp.bfloat16)
    low = (w - high.astype(jnp.float32)).astype(jnp.bfloat16)
    twice = jnp.concatenate([high, high], axis=1)
    scale = jnp.concatenate([s_ref[...], s_ref[...]], axis=0)

    def row(m):
        return jnp.concatenate(
            [ref[pl.ds(i * part + m, 8, stride=height), :] for ref in x_refs for i in range(ref.shape[0] // part)],
            axis=0,
        )

    for m in range(0, height, 2):
        x = jnp.concatenate([row(m), row(m + 1)], axis=1)
        x_high = x.astype(jnp.bfloat16)
        x_low = (x - x_high.astype(jnp.float32)).astype(jnp.bfloat16)
        mixed = jnp.dot(
            twice, jnp.concatenate([x_high, x_low], axis=0), preferred_element_type=jnp.float32
        ) + jnp.dot(low, x_high, preferred_element_type=jnp.float32)
        o_ref[pl.ds(m, n_freq, stride=height), :] = mixed[:, :LANES] * scale
        o_ref[pl.ds(m + 1, n_freq, stride=height), :] = mixed[:, LANES:] * scale


def body(green_tau, fit_matrix, aux_factors, freq_basis, screened, pair_mask):
    z, xl, c, y = (lax.axis_index(a) for a in ("z", "xl", "c", "y"))
    nz, ny = lax.axis_size("z"), lax.axis_size("y")
    times, n_rows, cols = green_tau.shape
    height, blocks = pair_mask.shape
    width = aux_factors.shape[0] // (2 * ny)
    part = times * height
    rows = 4 * part
    f32, bf16 = jnp.float32, jnp.bfloat16
    shape = jax.ShapeDtypeStruct

    def shift(v, axis, by):
        n = lax.axis_size(axis)
        return lax.ppermute(v, axis, [(i, (i + by) % n) for i in range(n)])

    exact = lax.Precision.HIGHEST
    order = jnp.stack([(z + nz - d) % nz for d in range(nz)])
    source = (order[:, None] * (4 * times) + jnp.arange(4 * times)[None, :]).reshape(1, -1)
    n_time = source.shape[1]
    pick = (jnp.arange(n_time)[:, None] == source).astype(f32)
    picked = jnp.dot(fit_matrix.astype(f32), pick, precision=exact)
    weights = jnp.dot(freq_basis, picked, precision=exact)
    at = jnp.stack([y, xl * 2 + c, z]).astype(jnp.int32)

    def stage(v, after):
        out = pl.pallas_call(
            stage_kernel,
            in_specs=[pl.BlockSpec(memory_space=pltpu.HBM), ANY],
            out_specs=WHOLE,
            out_shape=pltpu.VMEM(v.shape, v.dtype),
            scratch_shapes=[pltpu.SemaphoreType.DMA],
            compiler_params=SMALL,
            cost_estimate=COST,
        )(v, after)
        return pltpu.with_memory_space_constraint(out, pltpu.VMEM)

    def swap(v, e, f):
        pairs = [(i * 2 + j, (i ^ e) * 2 + (j ^ f)) for i in (0, 1) for j in (0, 1)]
        return lax.ppermute(v, ("xl", "c"), pairs)

    aux = stage(aux_factors.reshape(2, ny, width, cols), at)
    quad = pl.pallas_call(
        join_kernel,
        out_shape=shape((4, height, blocks), pair_mask.dtype),
        compiler_params=SMALL,
        cost_estimate=LITTLE,
    )(pair_mask, swap(pair_mask, 0, 1), swap(pair_mask, 1, 0), swap(pair_mask, 1, 1))
    marks = [quad if d == 0 else shift(quad, "z", -d) for d in range(nz)]
    green = stage(green_tau.reshape(times, n_rows // height, height, cols), quad)

    def call(kernel, after, extra, extra_specs, out_shape, cost=COST):
        fixed = lambda s: pl.BlockSpec(s.shape, lambda j, at: (0,) * len(s.shape))
        outs = out_shape if isinstance(out_shape, list) else [out_shape]
        got = pl.pallas_call(
            kernel,
            grid_spec=pltpu.PrefetchScalarGridSpec(
                num_scalar_prefetch=1,
                grid=(1,),
                in_specs=[WHOLE, WHOLE, ANY] + [s or fixed(v) for s, v in zip(extra_specs, extra, strict=True)],
                out_specs=[fixed(s) for s in outs],
                scratch_shapes=[pltpu.VMEM((rows, cols), bf16)],
            ),
            out_shape=outs,
            compiler_params=SMALL,
            cost_estimate=cost,
        )(at, green, aux, after, *extra)
        return got if isinstance(out_shape, list) else got[0]

    step1 = {}

    def far(chunks, after):
        out = shape((len(chunks), rows, width), bf16)
        lo, hi = call(
            functools.partial(far_kernel, chunks), after, [marks[d] for d in chunks], [None] * len(chunks), [out, out]
        )
        got = shift(lo, "y", -1), shift(hi, "y", 1)
        for q, d in enumerate(chunks):
            step1[d] = q, got
        return lo

    message = (4, 2, part, width)
    step2 = {}

    def near(d, after, arrived=(), cost=COST):
        q, got = step1[d]
        spec = pl.BlockSpec((1, rows, width), lambda j, at: (q, 0, 0))
        down, up = call(
            functools.partial(near_kernel, d), after, [marks[d], *got, *arrived],
            [None, spec, spec] + [ANY] * len(arrived),
            [shape(message, bf16), shape(message, bf16)], cost,
        )
        step2[d] = shift(down, "y", -1), shift(up, "y", 1)
        return down

    def own(after):
        joined = jnp.concatenate(marks)
        out = shape((nz, *message), f32)
        return pl.pallas_call(
            own_kernel,
            grid_spec=pltpu.PrefetchScalarGridSpec(
                num_scalar_prefetch=1,
                grid=(nz,),
                in_specs=[WHOLE, WHOLE, ANY, pl.BlockSpec((4, height, blocks), lambda j, at: (j, 0, 0))],
                out_specs=pl.BlockSpec((1, *message), lambda j, at: (j, 0, 0, 0, 0)),
                scratch_shapes=[pltpu.VMEM((rows, cols), bf16)],
            ),
            out_shape=out,
            compiler_params=SMALL,
            cost_estimate=COST,
        )(at, green, aux, after, joined)

    crossed = {}

    def cross(d, after, kind, cost=LITTLE):
        fixed = pl.BlockSpec(message, lambda j: (0, 0, 0, 0))
        total = pl.pallas_call(
            sum_kernel,
            grid=(1,),
            in_specs=[pl.BlockSpec((1, *message), lambda j: (d, 0, 0, 0, 0)), fixed, fixed, ANY],
            out_specs=fixed,
            out_shape=shape(message, kind),
            compiler_params=SMALL,
            cost_estimate=cost,
        )(mine, *step2[d], after)
        crossed[d] = lax.all_to_all(
            total.reshape(8, part, width), ("xl", "c", "xh"), split_axis=0, concat_axis=0, tiled=True
        )
        return total

    pieces = {}

    def gather(d, after):
        got = crossed[d]
        out = pl.pallas_call(
            gather_kernel,
            in_specs=[pl.BlockSpec(got.shape, lambda: (0, 0, 0)), ANY],
            out_shape=shape((rows, width), f32),
            compiler_params=SMALL,
            cost_estimate=LITTLE,
        )(got, after)
        pieces[d] = out if d == 0 else shift(out, "z", d)
        return out

    last = far((2, 0), quad)
    last = far((1, 3), last)
    last = near(2, last)
    last = mine = own(last)
    last = near(1, last)
    last = near(3, last, cost=LITTLE)
    last = near(0, last, step2[2], LITTLE)
    last = cross(2, last, f32)
    last = cross(1, last, bf16, LONG)
    last = gather(2, last)
    last = cross(3, last, bf16)
    last = gather(1, last)
    last = cross(0, last, bf16)
    last = gather(3, last)
    gather(0, last)

    n_freq = weights.shape[0]
    lane = lambda v: pl.BlockSpec((v.shape[0], LANES), lambda j: (0, j))
    held = [pieces[d] for d in range(nz)]
    sigma = pl.pallas_call(
        final_kernel,
        grid=(width // LANES,),
        in_specs=[pl.BlockSpec(weights.shape, lambda j: (0, 0))] + [lane(v) for v in (screened, *held)],
        out_specs=pl.BlockSpec((n_freq * height, LANES), lambda j: (0, j)),
        out_shape=shape((n_freq * height, width), f32),
        compiler_params=pltpu.CompilerParams(vmem_limit_bytes=28 * 2**20),
    )(weights, screened, *held)
    return sigma.reshape(n_freq, height, width)


def solution(mesh):
    devices = np.array(mesh.devices).reshape(4, 2, 2, 2, 4)
    fine = Mesh(devices, ("z", "xl", "c", "xh", "y"))
    tau, aux = ("z", "xl", "c"), ("xh", "y")
    return jax.shard_map(
        body,
        mesh=fine,
        in_specs=(P(tau, None, aux), P(), P(None, aux), P(), P(None, aux), P(tau, aux)),
        out_specs=P(None, tau, aux),
        check_vma=False,
    )
```

```python
import functools

import jax
import jax.numpy as jnp
import numpy as np
from jax import lax
from jax.experimental import pallas as pl
from jax.experimental.pallas import tpu as pltpu
from jax.sharding import Mesh, PartitionSpec as P

BLOCK = 128
LANES = 128
ANY = pl.BlockSpec(memory_space=pl.ANY)
WHOLE = pl.BlockSpec(memory_space=pltpu.VMEM)
SMALL = pltpu.CompilerParams(vmem_limit_bytes=14 * 2**20)
COST = pl.CostEstimate(flops=4 * 10**9, bytes_accessed=2 * 10**7, transcendentals=0)
LITTLE = pl.CostEstimate(flops=10**6, bytes_accessed=10**5, transcendentals=0)
LONG = pl.CostEstimate(flops=10**11, bytes_accessed=10**6, transcendentals=0)


def stage_kernel(source, after, held, sem):
    copy = pltpu.make_async_copy(source, held, sem)
    copy.start()
    copy.wait()


def join_kernel(a, b, c, d, out):
    for i, v in enumerate((a, b, c, d)):
        out[i] = v[...]


def fill(at, chunk, green_ref, mask_ref, rows_ref):
    times, _, height, cols = green_ref.shape
    base = lax.rem(at[2] + chunk, 4) * 4
    for i in range(4):
        marks = mask_ref[i ^ at[1]].astype(jnp.float32)
        for k in range(cols // BLOCK):
            keep = jnp.broadcast_to(marks[:, k : k + 1], (height, BLOCK)).astype(jnp.bfloat16)
            lanes = slice(k * BLOCK, (k + 1) * BLOCK)
            for t in range(times):
                row = (i * times + t) * height
                rows_ref[row : row + height, lanes] = green_ref[t, base + i, :, lanes] * keep


def product(rows_ref, a):
    return lax.dot_general(rows_ref[...], a, (((1,), (1,)), ((), ())), preferred_element_type=jnp.float32)


def put(out_ref, h, v):
    part = out_ref.shape[2]
    for i in range(4):
        out_ref[i, h] = v[i * part : (i + 1) * part].astype(out_ref.dtype)


def far_kernel(chunks, at, green_ref, aux_ref, after, *refs):
    mask_refs, (lo_ref, hi_ref, rows_ref) = refs[: len(chunks)], refs[-3:]
    target = lax.rem(at[0] + 2, aux_ref.shape[1])
    for q, chunk in enumerate(chunks):
        fill(at, chunk, green_ref, mask_refs[q], rows_ref)
        lo_ref[q] = product(rows_ref, aux_ref[0, target]).astype(jnp.bfloat16)
        hi_ref[q] = product(rows_ref, aux_ref[1, target]).astype(jnp.bfloat16)


def near_kernel(chunks, at, green_ref, aux_ref, after, *refs):
    rows_ref = refs[-1]
    n = aux_ref.shape[1]
    below, above = lax.rem(at[0] + n - 1, n), lax.rem(at[0] + 1, n)
    for q, chunk in enumerate(chunks):
        mask_ref, from_up, from_down = refs[3 * q : 3 * q + 3]
        down_ref, up_ref = refs[2 * q - 1 - 2 * len(chunks) :][:2]
        fill(at, chunk, green_ref, mask_ref, rows_ref)
        put(down_ref, 0, product(rows_ref, aux_ref[0, below]) + from_up[0].astype(jnp.float32))
        put(down_ref, 1, product(rows_ref, aux_ref[1, below]))
        put(up_ref, 0, product(rows_ref, aux_ref[0, above]))
        put(up_ref, 1, product(rows_ref, aux_ref[1, above]) + from_down[0].astype(jnp.float32))


def own_kernel(at, green_ref, aux_ref, after, mask_refs, out_ref, rows_ref):
    chunk = pl.program_id(0)
    fill(at, chunk, green_ref, mask_refs, rows_ref)
    for h in range(2):
        put(out_ref.at[0], h, product(rows_ref, aux_ref[h, at[0]]))


def sum_kernel(n, *refs):
    out_ref = refs[-1]
    for q in range(n):
        own_ref, from_up, from_down = refs[3 * q : 3 * q + 3]
        for i in range(4):
            for h in range(2):
                others = from_up[i, h].astype(jnp.float32) + from_down[i, h].astype(jnp.float32)
                out_ref[2 * i + h, q] = (own_ref[0, i, h] + others).astype(out_ref.dtype)


def gather_kernel(got_ref, after, *out_refs):
    part = got_ref.shape[2]
    for q, out_ref in enumerate(out_refs):
        for i in range(4):
            both = got_ref[2 * i, q].astype(jnp.float32) + got_ref[2 * i + 1, q].astype(jnp.float32)
            out_ref[i * part : (i + 1) * part] = both


def final_kernel(w_ref, s_ref, *refs):
    x_refs, o_ref = refs[:-1], refs[-1]
    n_freq, _ = w_ref.shape
    height = o_ref.shape[0] // n_freq
    part = 8 * height
    w = w_ref[...]
    high = w.astype(jnp.bfloat16)
    low = (w - high.astype(jnp.float32)).astype(jnp.bfloat16)
    twice = jnp.concatenate([high, high], axis=1)
    scale = jnp.concatenate([s_ref[...], s_ref[...]], axis=0)

    def row(m):
        return jnp.concatenate(
            [ref[pl.ds(i * part + m, 8, stride=height), :] for ref in x_refs for i in range(ref.shape[0] // part)],
            axis=0,
        )

    for m in range(0, height, 2):
        x = jnp.concatenate([row(m), row(m + 1)], axis=1)
        x_high = x.astype(jnp.bfloat16)
        x_low = (x - x_high.astype(jnp.float32)).astype(jnp.bfloat16)
        mixed = jnp.dot(
            twice, jnp.concatenate([x_high, x_low], axis=0), preferred_element_type=jnp.float32
        ) + jnp.dot(low, x_high, preferred_element_type=jnp.float32)
        o_ref[pl.ds(m, n_freq, stride=height), :] = mixed[:, :LANES] * scale
        o_ref[pl.ds(m + 1, n_freq, stride=height), :] = mixed[:, LANES:] * scale


def body(green_tau, fit_matrix, aux_factors, freq_basis, screened, pair_mask):
    z, xl, c, y = (lax.axis_index(a) for a in ("z", "xl", "c", "y"))
    nz, ny = lax.axis_size("z"), lax.axis_size("y")
    times, n_rows, cols = green_tau.shape
    height, blocks = pair_mask.shape
    width = aux_factors.shape[0] // (2 * ny)
    part = times * height
    rows = 4 * part
    f32, bf16 = jnp.float32, jnp.bfloat16
    shape = jax.ShapeDtypeStruct

    def shift(v, axis, by):
        n = lax.axis_size(axis)
        return lax.ppermute(v, axis, [(i, (i + by) % n) for i in range(n)])

    exact = lax.Precision.HIGHEST
    order = jnp.stack([(z + nz - d) % nz for d in range(nz)])
    source = (order[:, None] * (4 * times) + jnp.arange(4 * times)[None, :]).reshape(1, -1)
    n_time = source.shape[1]
    pick = (jnp.arange(n_time)[:, None] == source).astype(f32)
    picked = jnp.dot(fit_matrix.astype(f32), pick, precision=exact)
    weights = jnp.dot(freq_basis, picked, precision=exact)
    at = jnp.stack([y, xl * 2 + c, z]).astype(jnp.int32)

    def stage(v, after):
        out = pl.pallas_call(
            stage_kernel,
            in_specs=[pl.BlockSpec(memory_space=pltpu.HBM), ANY],
            out_specs=WHOLE,
            out_shape=pltpu.VMEM(v.shape, v.dtype),
            scratch_shapes=[pltpu.SemaphoreType.DMA],
            compiler_params=SMALL,
            cost_estimate=COST,
        )(v, after)
        return pltpu.with_memory_space_constraint(out, pltpu.VMEM)

    def swap(v, e, f):
        pairs = [(i * 2 + j, (i ^ e) * 2 + (j ^ f)) for i in (0, 1) for j in (0, 1)]
        return lax.ppermute(v, ("xl", "c"), pairs)

    quad = pl.pallas_call(
        join_kernel,
        out_shape=shape((4, height, blocks), pair_mask.dtype),
        compiler_params=SMALL,
        cost_estimate=LITTLE,
    )(pair_mask, swap(pair_mask, 0, 1), swap(pair_mask, 1, 0), swap(pair_mask, 1, 1))
    marks = [quad if d == 0 else shift(quad, "z", -d) for d in range(nz)]
    aux = stage(aux_factors.reshape(2, ny, width, cols), quad)
    green = stage(green_tau.reshape(times, n_rows // height, height, cols), quad)

    def call(kernel, after, extra, extra_specs, out_shape, cost=COST):
        fixed = lambda s: pl.BlockSpec(s.shape, lambda j, at: (0,) * len(s.shape))
        outs = out_shape if isinstance(out_shape, list) else [out_shape]
        got = pl.pallas_call(
            kernel,
            grid_spec=pltpu.PrefetchScalarGridSpec(
                num_scalar_prefetch=1,
                grid=(1,),
                in_specs=[WHOLE, WHOLE, ANY] + [s or fixed(v) for s, v in zip(extra_specs, extra, strict=True)],
                out_specs=[fixed(s) for s in outs],
                scratch_shapes=[pltpu.VMEM((rows, cols), bf16)],
            ),
            out_shape=outs,
            compiler_params=SMALL,
            cost_estimate=cost,
        )(at, green, aux, after, *extra)
        return got if isinstance(out_shape, list) else got[0]

    step1 = {}

    def far(chunks, after, arrived=()):
        out = shape((len(chunks), rows, width), bf16)
        lo, hi = call(
            functools.partial(far_kernel, chunks), after,
            [*(marks[d] for d in chunks), *arrived], [None] * len(chunks) + [ANY] * len(arrived), [out, out],
        )
        got = shift(lo, "y", -1), shift(hi, "y", 1)
        for q, d in enumerate(chunks):
            step1[d] = q, got
        return lo

    message = (4, 2, part, width)
    step2 = {}

    def near(chunks, after, arrived=(), cost=COST):
        args, specs = [], []
        for d in chunks:
            q, got = step1[d]
            spec = pl.BlockSpec((1, rows, width), lambda j, at, q=q: (q, 0, 0))
            args += [marks[d], *got]
            specs += [None, spec, spec]
        out = call(
            functools.partial(near_kernel, chunks), after, args + [*arrived], specs + [ANY] * len(arrived),
            [shape(message, bf16)] * (2 * len(chunks)), cost,
        )
        for k, d in enumerate(chunks):
            step2[d] = shift(out[2 * k], "y", -1), shift(out[2 * k + 1], "y", 1)
        return out[0]

    def own(after):
        joined = jnp.concatenate(marks)
        return pl.pallas_call(
            own_kernel,
            grid_spec=pltpu.PrefetchScalarGridSpec(
                num_scalar_prefetch=1,
                grid=(nz,),
                in_specs=[WHOLE, WHOLE, ANY, pl.BlockSpec((4, height, blocks), lambda j, at: (j, 0, 0))],
                out_specs=pl.BlockSpec((1, *message), lambda j, at: (j, 0, 0, 0, 0)),
                scratch_shapes=[pltpu.VMEM((rows, cols), bf16)],
            ),
            out_shape=pltpu.HBM((nz, *message), f32),
            compiler_params=SMALL,
            cost_estimate=COST,
        )(at, green, aux, after, joined)

    crossed = {}

    def cross(chunks, after, kind, cost=LITTLE):
        n = len(chunks)
        fixed = pl.BlockSpec(message, lambda j: (0, 0, 0, 0))
        own_of = lambda d: pl.BlockSpec((1, *message), lambda j: (d, 0, 0, 0, 0))
        total = pl.pallas_call(
            functools.partial(sum_kernel, n),
            grid=(1,),
            in_specs=[v for d in chunks for v in (own_of(d), fixed, fixed)] + [ANY],
            out_specs=pl.BlockSpec((8, n, part, width), lambda j: (0, 0, 0, 0)),
            out_shape=shape((8, n, part, width), kind),
            compiler_params=SMALL,
            cost_estimate=cost,
        )(*[v for d in chunks for v in (mine, *step2[d])], after)
        crossed[chunks] = lax.all_to_all(total, ("xl", "c", "xh"), split_axis=0, concat_axis=0, tiled=True)
        return total

    pieces = {}

    def gather(chunks, after):
        got = crossed[chunks]
        outs = pl.pallas_call(
            gather_kernel,
            in_specs=[pl.BlockSpec(got.shape, lambda: (0, 0, 0, 0)), ANY],
            out_shape=[shape((rows, width), f32)] * len(chunks),
            compiler_params=SMALL,
            cost_estimate=LITTLE,
        )(got, after)
        for d, out in zip(chunks, outs, strict=True):
            pieces[d] = out if d == 0 else shift(out, "z", d)
        return outs[0]

    last = far((2, 0), quad, (marks[1], marks[3]))
    last = far((1, 3), last)
    last = near((2,), last)
    last = mine = own(last)
    mine = pltpu.with_memory_space_constraint(mine, pltpu.HBM)
    last = near((1,), last)
    last = near((3, 0), last, cost=LITTLE)
    last = cross((2,), last, f32)
    last = cross((1, 3), last, bf16, LONG)
    last = gather((2,), last)
    last = cross((0,), last, bf16, LONG)
    last = gather((1, 3), last)
    gather((0,), last)

    n_freq = weights.shape[0]
    lane = lambda v: pl.BlockSpec((v.shape[0], LANES), lambda j: (0, j))
    held = [pieces[d] for d in range(nz)]
    sigma = pl.pallas_call(
        final_kernel,
        grid=(width // LANES,),
        in_specs=[pl.BlockSpec(weights.shape, lambda j: (0, 0))] + [lane(v) for v in (screened, *held)],
        out_specs=pl.BlockSpec((n_freq * height, LANES), lambda j: (0, j)),
        out_shape=shape((n_freq * height, width), f32),
        compiler_params=pltpu.CompilerParams(vmem_limit_bytes=28 * 2**20),
    )(weights, screened, *held)
    return sigma.reshape(n_freq, height, width)


def solution(mesh):
    devices = np.array(mesh.devices).reshape(4, 2, 2, 2, 4)
    fine = Mesh(devices, ("z", "xl", "c", "xh", "y"))
    tau, aux = ("z", "xl", "c"), ("xh", "y")
    return jax.shard_map(
        body,
        mesh=fine,
        in_specs=(P(tau, None, aux), P(), P(None, aux), P(), P(None, aux), P(tau, aux)),
        out_specs=P(None, tau, aux),
        check_vma=False,
    )
```

```python
import functools

import jax
import jax.numpy as jnp
import numpy as np
from jax import lax
from jax.experimental import pallas as pl
from jax.experimental.pallas import tpu as pltpu
from jax.sharding import Mesh, PartitionSpec as P

BLOCK = 128
LANES = 128
ANY = pl.BlockSpec(memory_space=pl.ANY)
WHOLE = pl.BlockSpec(memory_space=pltpu.VMEM)
SMALL = pltpu.CompilerParams(vmem_limit_bytes=14 * 2**20)
COST = pl.CostEstimate(flops=4 * 10**9, bytes_accessed=2 * 10**7, transcendentals=0)
LITTLE = pl.CostEstimate(flops=10**6, bytes_accessed=10**5, transcendentals=0)
LONG = pl.CostEstimate(flops=10**11, bytes_accessed=10**6, transcendentals=0)


def stage_kernel(source, after, held, sem):
    copy = pltpu.make_async_copy(source, held, sem)
    copy.start()
    copy.wait()


def join_kernel(a, b, c, d, out):
    for i, v in enumerate((a, b, c, d)):
        out[i] = v[...]


def fill(at, chunk, green_ref, mask_ref, rows_ref):
    times, _, height, cols = green_ref.shape
    base = lax.rem(at[2] + chunk, 4) * 4
    for i in range(4):
        marks = mask_ref[i ^ at[1]].astype(jnp.float32)
        for k in range(cols // BLOCK):
            keep = jnp.broadcast_to(marks[:, k : k + 1], (height, BLOCK)).astype(jnp.bfloat16)
            lanes = slice(k * BLOCK, (k + 1) * BLOCK)
            for t in range(times):
                row = (i * times + t) * height
                rows_ref[row : row + height, lanes] = green_ref[t, base + i, :, lanes] * keep


def product(rows_ref, a):
    return lax.dot_general(rows_ref[...], a, (((1,), (1,)), ((), ())), preferred_element_type=jnp.float32)


def put(out_ref, h, v):
    part = out_ref.shape[2]
    for i in range(4):
        out_ref[i, h] = v[i * part : (i + 1) * part].astype(out_ref.dtype)


def far_kernel(chunks, at, green_ref, aux_ref, after, *refs):
    mask_refs, (lo_ref, hi_ref, rows_ref) = refs[: len(chunks)], refs[-3:]
    target = lax.rem(at[0] + 2, aux_ref.shape[1])
    for q, chunk in enumerate(chunks):
        fill(at, chunk, green_ref, mask_refs[q], rows_ref)
        lo_ref[q] = product(rows_ref, aux_ref[0, target]).astype(jnp.bfloat16)
        hi_ref[q] = product(rows_ref, aux_ref[1, target]).astype(jnp.bfloat16)


def near_kernel(chunks, at, green_ref, aux_ref, after, *refs):
    rows_ref = refs[-1]
    n = aux_ref.shape[1]
    below, above = lax.rem(at[0] + n - 1, n), lax.rem(at[0] + 1, n)
    for q, chunk in enumerate(chunks):
        mask_ref, from_up, from_down = refs[3 * q : 3 * q + 3]
        down_ref, up_ref = refs[2 * q - 1 - 2 * len(chunks) :][:2]
        fill(at, chunk, green_ref, mask_ref, rows_ref)
        put(down_ref, 0, product(rows_ref, aux_ref[0, below]) + from_up[0].astype(jnp.float32))
        put(down_ref, 1, product(rows_ref, aux_ref[1, below]))
        put(up_ref, 0, product(rows_ref, aux_ref[0, above]))
        put(up_ref, 1, product(rows_ref, aux_ref[1, above]) + from_down[0].astype(jnp.float32))


def own_kernel(at, green_ref, aux_ref, after, mask_refs, out_ref, rows_ref):
    chunk = pl.program_id(0)
    fill(at, chunk, green_ref, mask_refs, rows_ref)
    for h in range(2):
        put(out_ref.at[0], h, product(rows_ref, aux_ref[h, at[0]]))


def sum_kernel(n, *refs):
    out_ref = refs[-1]
    for q in range(n):
        own_ref, from_up, from_down = refs[3 * q : 3 * q + 3]
        for i in range(4):
            for h in range(2):
                others = from_up[i, h].astype(jnp.float32) + from_down[i, h].astype(jnp.float32)
                out_ref[2 * i + h, q] = (own_ref[0, i, h] + others).astype(out_ref.dtype)


def gather_kernel(got_ref, after, *out_refs):
    part = got_ref.shape[2]
    for q, out_ref in enumerate(out_refs):
        for i in range(4):
            both = got_ref[2 * i, q].astype(jnp.float32) + got_ref[2 * i + 1, q].astype(jnp.float32)
            out_ref[i * part : (i + 1) * part] = both


def final_kernel(w_ref, s_ref, *refs):
    x_refs, o_ref = refs[:-1], refs[-1]
    n_freq, _ = w_ref.shape
    height = o_ref.shape[0] // n_freq
    part = 8 * height
    w = w_ref[...]
    high = w.astype(jnp.bfloat16)
    low = (w - high.astype(jnp.float32)).astype(jnp.bfloat16)
    twice = jnp.concatenate([high, high], axis=1)
    scale = jnp.concatenate([s_ref[...], s_ref[...]], axis=0)

    def row(m):
        return jnp.concatenate(
            [ref[pl.ds(i * part + m, 8, stride=height), :] for ref in x_refs for i in range(ref.shape[0] // part)],
            axis=0,
        )

    for m in range(0, height, 2):
        x = jnp.concatenate([row(m), row(m + 1)], axis=1)
        x_high = x.astype(jnp.bfloat16)
        x_low = (x - x_high.astype(jnp.float32)).astype(jnp.bfloat16)
        mixed = jnp.dot(
            twice, jnp.concatenate([x_high, x_low], axis=0), preferred_element_type=jnp.float32
        ) + jnp.dot(low, x_high, preferred_element_type=jnp.float32)
        o_ref[pl.ds(m, n_freq, stride=height), :] = mixed[:, :LANES] * scale
        o_ref[pl.ds(m + 1, n_freq, stride=height), :] = mixed[:, LANES:] * scale


def body(green_tau, fit_matrix, aux_factors, freq_basis, screened, pair_mask):
    z, xl, c, y = (lax.axis_index(a) for a in ("z", "xl", "c", "y"))
    nz, ny = lax.axis_size("z"), lax.axis_size("y")
    times, n_rows, cols = green_tau.shape
    height, blocks = pair_mask.shape
    width = aux_factors.shape[0] // (2 * ny)
    part = times * height
    rows = 4 * part
    f32, bf16 = jnp.float32, jnp.bfloat16
    shape = jax.ShapeDtypeStruct

    def shift(v, axis, by):
        n = lax.axis_size(axis)
        return lax.ppermute(v, axis, [(i, (i + by) % n) for i in range(n)])

    exact = lax.Precision.HIGHEST
    order = jnp.stack([(z + nz - d) % nz for d in range(nz)])
    source = (order[:, None] * (4 * times) + jnp.arange(4 * times)[None, :]).reshape(1, -1)
    n_time = source.shape[1]
    pick = (jnp.arange(n_time)[:, None] == source).astype(f32)
    picked = jnp.dot(fit_matrix.astype(f32), pick, precision=exact)
    weights = jnp.dot(freq_basis, picked, precision=exact)
    at = jnp.stack([y, xl * 2 + c, z]).astype(jnp.int32)

    def stage(v, after):
        out = pl.pallas_call(
            stage_kernel,
            in_specs=[pl.BlockSpec(memory_space=pltpu.HBM), ANY],
            out_specs=WHOLE,
            out_shape=pltpu.VMEM(v.shape, v.dtype),
            scratch_shapes=[pltpu.SemaphoreType.DMA],
            compiler_params=SMALL,
            cost_estimate=COST,
        )(v, after)
        return pltpu.with_memory_space_constraint(out, pltpu.VMEM)

    def swap(v, e, f):
        pairs = [(i * 2 + j, (i ^ e) * 2 + (j ^ f)) for i in (0, 1) for j in (0, 1)]
        return lax.ppermute(v, ("xl", "c"), pairs)

    aux = stage(aux_factors.reshape(2, ny, width, cols), at)
    quad = pl.pallas_call(
        join_kernel,
        out_shape=shape((4, height, blocks), pair_mask.dtype),
        compiler_params=SMALL,
        cost_estimate=LITTLE,
    )(pair_mask, swap(pair_mask, 0, 1), swap(pair_mask, 1, 0), swap(pair_mask, 1, 1))
    marks = [quad if d == 0 else shift(quad, "z", -d) for d in range(nz)]
    green = stage(green_tau.reshape(times, n_rows // height, height, cols), quad)

    def call(kernel, after, extra, extra_specs, out_shape, cost=COST):
        fixed = lambda s: pl.BlockSpec(s.shape, lambda j, at: (0,) * len(s.shape))
        outs = out_shape if isinstance(out_shape, list) else [out_shape]
        got = pl.pallas_call(
            kernel,
            grid_spec=pltpu.PrefetchScalarGridSpec(
                num_scalar_prefetch=1,
                grid=(1,),
                in_specs=[WHOLE, WHOLE, ANY] + [s or fixed(v) for s, v in zip(extra_specs, extra, strict=True)],
                out_specs=[fixed(s) for s in outs],
                scratch_shapes=[pltpu.VMEM((rows, cols), bf16)],
            ),
            out_shape=outs,
            compiler_params=SMALL,
            cost_estimate=cost,
        )(at, green, aux, after, *extra)
        return got if isinstance(out_shape, list) else got[0]

    step1 = {}

    def far(chunks, after, arrived=()):
        out = shape((len(chunks), rows, width), bf16)
        lo, hi = call(
            functools.partial(far_kernel, chunks), after,
            [*(marks[d] for d in chunks), *arrived], [None] * len(chunks) + [ANY] * len(arrived), [out, out],
        )
        got = shift(lo, "y", -1), shift(hi, "y", 1)
        for q, d in enumerate(chunks):
            step1[d] = q, got
        return lo

    message = (4, 2, part, width)
    step2 = {}

    def near(chunks, after, arrived=(), cost=COST):
        args, specs = [], []
        for d in chunks:
            q, got = step1[d]
            spec = pl.BlockSpec((1, rows, width), lambda j, at, q=q: (q, 0, 0))
            args += [marks[d], *got]
            specs += [None, spec, spec]
        out = call(
            functools.partial(near_kernel, chunks), after, args + [*arrived], specs + [ANY] * len(arrived),
            [shape(message, bf16)] * (2 * len(chunks)), cost,
        )
        for k, d in enumerate(chunks):
            step2[d] = shift(out[2 * k], "y", -1), shift(out[2 * k + 1], "y", 1)
        return out[0]

    def own(after):
        joined = jnp.concatenate(marks)
        return pl.pallas_call(
            own_kernel,
            grid_spec=pltpu.PrefetchScalarGridSpec(
                num_scalar_prefetch=1,
                grid=(nz,),
                in_specs=[WHOLE, WHOLE, ANY, pl.BlockSpec((4, height, blocks), lambda j, at: (j, 0, 0))],
                out_specs=pl.BlockSpec((1, *message), lambda j, at: (j, 0, 0, 0, 0)),
                scratch_shapes=[pltpu.VMEM((rows, cols), bf16)],
            ),
            out_shape=pltpu.HBM((nz, *message), f32),
            compiler_params=SMALL,
            cost_estimate=COST,
        )(at, green, aux, after, joined)

    crossed = {}

    def cross(chunks, after, kind, cost=LITTLE):
        n = len(chunks)
        fixed = pl.BlockSpec(message, lambda j: (0, 0, 0, 0))
        own_of = lambda d: pl.BlockSpec((1, *message), lambda j: (d, 0, 0, 0, 0))
        total = pl.pallas_call(
            functools.partial(sum_kernel, n),
            grid=(1,),
            in_specs=[v for d in chunks for v in (own_of(d), fixed, fixed)] + [ANY],
            out_specs=pl.BlockSpec((8, n, part, width), lambda j: (0, 0, 0, 0)),
            out_shape=shape((8, n, part, width), kind),
            compiler_params=SMALL,
            cost_estimate=cost,
        )(*[v for d in chunks for v in (mine, *step2[d])], after)
        crossed[chunks] = lax.all_to_all(total, ("xl", "c", "xh"), split_axis=0, concat_axis=0, tiled=True)
        return total

    pieces = {}

    def gather(chunks, after):
        got = crossed[chunks]
        outs = pl.pallas_call(
            gather_kernel,
            in_specs=[pl.BlockSpec(got.shape, lambda: (0, 0, 0, 0)), ANY],
            out_shape=[shape((rows, width), f32)] * len(chunks),
            compiler_params=SMALL,
            cost_estimate=LITTLE,
        )(got, after)
        for d, out in zip(chunks, outs, strict=True):
            pieces[d] = out if d == 0 else shift(out, "z", d)
        return outs[0]

    last = far((2, 0), quad, (marks[1], marks[3]))
    last = far((1, 3), last)
    last = near((2,), last)
    last = mine = own(last)
    mine = pltpu.with_memory_space_constraint(mine, pltpu.HBM)
    last = near((1,), last)
    last = near((3, 0), last, step2[2], LITTLE)
    last = cross((2,), last, f32)
    last = cross((1, 3), last, bf16, LONG)
    last = gather((2,), last)
    last = cross((0,), last, bf16, LONG)
    last = gather((1, 3), last)
    gather((0,), last)

    n_freq = weights.shape[0]
    lane = lambda v: pl.BlockSpec((v.shape[0], LANES), lambda j: (0, j))
    held = [pieces[d] for d in range(nz)]
    sigma = pl.pallas_call(
        final_kernel,
        grid=(width // LANES,),
        in_specs=[pl.BlockSpec(weights.shape, lambda j: (0, 0))] + [lane(v) for v in (screened, *held)],
        out_specs=pl.BlockSpec((n_freq * height, LANES), lambda j: (0, j)),
        out_shape=shape((n_freq * height, width), f32),
        compiler_params=pltpu.CompilerParams(vmem_limit_bytes=28 * 2**20),
    )(weights, screened, *held)
    return sigma.reshape(n_freq, height, width)


def solution(mesh):
    devices = np.array(mesh.devices).reshape(4, 2, 2, 2, 4)
    fine = Mesh(devices, ("z", "xl", "c", "xh", "y"))
    tau, aux = ("z", "xl", "c"), ("xh", "y")
    return jax.shard_map(
        body,
        mesh=fine,
        in_specs=(P(tau, None, aux), P(), P(None, aux), P(), P(None, aux), P(tau, aux)),
        out_specs=P(None, tau, aux),
        check_vma=False,
    )
```

```python
import functools

import jax
import jax.numpy as jnp
import numpy as np
from jax import lax
from jax.experimental import pallas as pl
from jax.experimental.pallas import tpu as pltpu
from jax.sharding import Mesh, PartitionSpec as P

BLOCK = 128
LANES = 128
ANY = pl.BlockSpec(memory_space=pl.ANY)
WHOLE = pl.BlockSpec(memory_space=pltpu.VMEM)
SMALL = pltpu.CompilerParams(vmem_limit_bytes=14 * 2**20)
COST = pl.CostEstimate(flops=4 * 10**9, bytes_accessed=2 * 10**7, transcendentals=0)
LITTLE = pl.CostEstimate(flops=10**6, bytes_accessed=10**5, transcendentals=0)
LONG = pl.CostEstimate(flops=10**11, bytes_accessed=10**6, transcendentals=0)


def stage_kernel(source, after, held, sem):
    copy = pltpu.make_async_copy(source, held, sem)
    copy.start()
    copy.wait()


def join_kernel(a, b, c, d, out):
    for i, v in enumerate((a, b, c, d)):
        out[i] = v[...]


def fill(at, chunk, green_ref, mask_ref, rows_ref):
    times, _, height, cols = green_ref.shape
    base = lax.rem(at[2] + chunk, 4) * 4
    for i in range(4):
        marks = mask_ref[i ^ at[1]].astype(jnp.float32)
        for k in range(cols // BLOCK):
            keep = jnp.broadcast_to(marks[:, k : k + 1], (height, BLOCK)).astype(jnp.bfloat16)
            lanes = slice(k * BLOCK, (k + 1) * BLOCK)
            for t in range(times):
                row = (i * times + t) * height
                rows_ref[row : row + height, lanes] = green_ref[t, base + i, :, lanes] * keep


def product(rows_ref, a):
    return lax.dot_general(rows_ref[...], a, (((1,), (1,)), ((), ())), preferred_element_type=jnp.float32)


def put(out_ref, h, v):
    part = out_ref.shape[2]
    for i in range(4):
        out_ref[i, h] = v[i * part : (i + 1) * part].astype(out_ref.dtype)


def far_kernel(chunks, at, green_ref, aux_ref, after, *refs):
    mask_refs, (lo_ref, hi_ref, rows_ref) = refs[: len(chunks)], refs[-3:]
    target = lax.rem(at[0] + 2, aux_ref.shape[1])
    for q, chunk in enumerate(chunks):
        fill(at, chunk, green_ref, mask_refs[q], rows_ref)
        lo_ref[q] = product(rows_ref, aux_ref[0, target]).astype(jnp.bfloat16)
        hi_ref[q] = product(rows_ref, aux_ref[1, target]).astype(jnp.bfloat16)


def near_kernel(chunks, at, green_ref, aux_ref, after, *refs):
    rows_ref = refs[-1]
    n = aux_ref.shape[1]
    below, above = lax.rem(at[0] + n - 1, n), lax.rem(at[0] + 1, n)
    for q, chunk in enumerate(chunks):
        mask_ref, from_up, from_down = refs[3 * q : 3 * q + 3]
        down_ref, up_ref = refs[2 * q - 1 - 2 * len(chunks) :][:2]
        fill(at, chunk, green_ref, mask_ref, rows_ref)
        put(down_ref, 0, product(rows_ref, aux_ref[0, below]) + from_up[0].astype(jnp.float32))
        put(down_ref, 1, product(rows_ref, aux_ref[1, below]))
        put(up_ref, 0, product(rows_ref, aux_ref[0, above]))
        put(up_ref, 1, product(rows_ref, aux_ref[1, above]) + from_down[0].astype(jnp.float32))


def own_kernel(chunks, at, green_ref, aux_ref, after, *refs):
    n, rows_ref = len(chunks), refs[-1]
    for q, chunk in enumerate(chunks):
        fill(at, chunk, green_ref, refs[q], rows_ref)
        for h in range(2):
            put(refs[n + q], h, product(rows_ref, aux_ref[h, at[0]]))


def sum_kernel(n, *refs):
    out_ref = refs[-1]
    for q in range(n):
        own_ref, from_up, from_down = refs[3 * q : 3 * q + 3]
        for i in range(4):
            for h in range(2):
                others = from_up[i, h].astype(jnp.float32) + from_down[i, h].astype(jnp.float32)
                out_ref[2 * i + h, q] = (own_ref[i, h] + others).astype(out_ref.dtype)


def gather_kernel(got_ref, after, *out_refs):
    part = got_ref.shape[2]
    for q, out_ref in enumerate(out_refs):
        for i in range(4):
            both = got_ref[2 * i, q].astype(jnp.float32) + got_ref[2 * i + 1, q].astype(jnp.float32)
            out_ref[i * part : (i + 1) * part] = both


def final_kernel(w_ref, s_ref, *refs):
    x_refs, o_ref = refs[:-1], refs[-1]
    n_freq, _ = w_ref.shape
    height = o_ref.shape[0] // n_freq
    part = 8 * height
    w = w_ref[...]
    high = w.astype(jnp.bfloat16)
    low = (w - high.astype(jnp.float32)).astype(jnp.bfloat16)
    twice = jnp.concatenate([high, high], axis=1)
    scale = jnp.concatenate([s_ref[...], s_ref[...]], axis=0)

    def row(m):
        return jnp.concatenate(
            [ref[pl.ds(i * part + m, 8, stride=height), :] for ref in x_refs for i in range(ref.shape[0] // part)],
            axis=0,
        )

    for m in range(0, height, 2):
        x = jnp.concatenate([row(m), row(m + 1)], axis=1)
        x_high = x.astype(jnp.bfloat16)
        x_low = (x - x_high.astype(jnp.float32)).astype(jnp.bfloat16)
        mixed = jnp.dot(
            twice, jnp.concatenate([x_high, x_low], axis=0), preferred_element_type=jnp.float32
        ) + jnp.dot(low, x_high, preferred_element_type=jnp.float32)
        o_ref[pl.ds(m, n_freq, stride=height), :] = mixed[:, :LANES] * scale
        o_ref[pl.ds(m + 1, n_freq, stride=height), :] = mixed[:, LANES:] * scale


def body(green_tau, fit_matrix, aux_factors, freq_basis, screened, pair_mask):
    z, xl, c, y = (lax.axis_index(a) for a in ("z", "xl", "c", "y"))
    nz, ny = lax.axis_size("z"), lax.axis_size("y")
    times, n_rows, cols = green_tau.shape
    height, blocks = pair_mask.shape
    width = aux_factors.shape[0] // (2 * ny)
    part = times * height
    rows = 4 * part
    f32, bf16 = jnp.float32, jnp.bfloat16
    shape = jax.ShapeDtypeStruct

    def shift(v, axis, by):
        n = lax.axis_size(axis)
        return lax.ppermute(v, axis, [(i, (i + by) % n) for i in range(n)])

    exact = lax.Precision.HIGHEST
    order = jnp.stack([(z + nz - d) % nz for d in range(nz)])
    source = (order[:, None] * (4 * times) + jnp.arange(4 * times)[None, :]).reshape(1, -1)
    n_time = source.shape[1]
    pick = (jnp.arange(n_time)[:, None] == source).astype(f32)
    picked = jnp.dot(fit_matrix.astype(f32), pick, precision=exact)
    weights = jnp.dot(freq_basis, picked, precision=exact)
    at = jnp.stack([y, xl * 2 + c, z]).astype(jnp.int32)

    def stage(v, after):
        out = pl.pallas_call(
            stage_kernel,
            in_specs=[pl.BlockSpec(memory_space=pltpu.HBM), ANY],
            out_specs=WHOLE,
            out_shape=pltpu.VMEM(v.shape, v.dtype),
            scratch_shapes=[pltpu.SemaphoreType.DMA],
            compiler_params=SMALL,
            cost_estimate=COST,
        )(v, after)
        return pltpu.with_memory_space_constraint(out, pltpu.VMEM)

    def swap(v, e, f):
        pairs = [(i * 2 + j, (i ^ e) * 2 + (j ^ f)) for i in (0, 1) for j in (0, 1)]
        return lax.ppermute(v, ("xl", "c"), pairs)

    aux = stage(aux_factors.reshape(2, ny, width, cols), at)
    quad = pl.pallas_call(
        join_kernel,
        out_shape=shape((4, height, blocks), pair_mask.dtype),
        compiler_params=SMALL,
        cost_estimate=LITTLE,
    )(pair_mask, swap(pair_mask, 0, 1), swap(pair_mask, 1, 0), swap(pair_mask, 1, 1))
    marks = [quad if d == 0 else shift(quad, "z", -d) for d in range(nz)]
    green = stage(green_tau.reshape(times, n_rows // height, height, cols), quad)

    def call(kernel, after, extra, extra_specs, out_shape, cost=COST):
        fixed = lambda s: pl.BlockSpec(s.shape, lambda j, at: (0,) * len(s.shape))
        outs = out_shape if isinstance(out_shape, list) else [out_shape]
        got = pl.pallas_call(
            kernel,
            grid_spec=pltpu.PrefetchScalarGridSpec(
                num_scalar_prefetch=1,
                grid=(1,),
                in_specs=[WHOLE, WHOLE, ANY] + [s or fixed(v) for s, v in zip(extra_specs, extra, strict=True)],
                out_specs=[fixed(s) for s in outs],
                scratch_shapes=[pltpu.VMEM((rows, cols), bf16)],
            ),
            out_shape=outs,
            compiler_params=SMALL,
            cost_estimate=cost,
        )(at, green, aux, after, *extra)
        return got if isinstance(out_shape, list) else got[0]

    step1 = {}

    def far(chunks, after, arrived=()):
        out = shape((len(chunks), rows, width), bf16)
        lo, hi = call(
            functools.partial(far_kernel, chunks), after,
            [*(marks[d] for d in chunks), *arrived], [None] * len(chunks) + [ANY] * len(arrived), [out, out],
        )
        got = shift(lo, "y", -1), shift(hi, "y", 1)
        for q, d in enumerate(chunks):
            step1[d] = q, got
        return lo

    message = (4, 2, part, width)
    step2 = {}

    def near(chunks, after, arrived=(), cost=COST):
        args, specs = [], []
        for d in chunks:
            q, got = step1[d]
            spec = pl.BlockSpec((1, rows, width), lambda j, at, q=q: (q, 0, 0))
            args += [marks[d], *got]
            specs += [None, spec, spec]
        out = call(
            functools.partial(near_kernel, chunks), after, args + [*arrived], specs + [ANY] * len(arrived),
            [shape(message, bf16)] * (2 * len(chunks)), cost,
        )
        for k, d in enumerate(chunks):
            step2[d] = shift(out[2 * k], "y", -1), shift(out[2 * k + 1], "y", 1)
        return out[0]

    def own(after):
        chunks = tuple(range(nz))
        return call(
            functools.partial(own_kernel, chunks), after, [marks[d] for d in chunks], [None] * nz,
            [shape(message, f32)] * nz,
        )

    crossed = {}

    def cross(chunks, after, kind, cost=LITTLE):
        n = len(chunks)
        fixed = pl.BlockSpec(message, lambda j: (0, 0, 0, 0))
        total = pl.pallas_call(
            functools.partial(sum_kernel, n),
            grid=(1,),
            in_specs=[fixed] * (3 * n) + [ANY],
            out_specs=pl.BlockSpec((8, n, part, width), lambda j: (0, 0, 0, 0)),
            out_shape=shape((8, n, part, width), kind),
            compiler_params=SMALL,
            cost_estimate=cost,
        )(*[v for d in chunks for v in (mine[d], *step2[d])], after)
        crossed[chunks] = lax.all_to_all(total, ("xl", "c", "xh"), split_axis=0, concat_axis=0, tiled=True)
        return total

    pieces = {}

    def gather(chunks, after):
        got = crossed[chunks]
        outs = pl.pallas_call(
            gather_kernel,
            in_specs=[pl.BlockSpec(got.shape, lambda: (0, 0, 0, 0)), ANY],
            out_shape=[shape((rows, width), f32)] * len(chunks),
            compiler_params=SMALL,
            cost_estimate=LITTLE,
        )(got, after)
        for d, out in zip(chunks, outs, strict=True):
            pieces[d] = out if d == 0 else shift(out, "z", d)
        return outs[0]

    last = far((2, 0), quad, (marks[1], marks[3]))
    last = far((1, 3), last)
    mine = own(last)
    last = near((2,), mine[0])
    last = near((1,), last)
    last = near((3, 0), last, step2[2], LITTLE)
    last = cross((2,), last, f32)
    last = cross((1, 3), last, bf16, LONG)
    last = gather((2,), last)
    last = cross((0,), last, bf16, LONG)
    last = gather((1, 3), last)
    gather((0,), last)

    n_freq = weights.shape[0]
    lane = lambda v: pl.BlockSpec((v.shape[0], LANES), lambda j: (0, j))
    held = [pieces[d] for d in range(nz)]
    sigma = pl.pallas_call(
        final_kernel,
        grid=(width // LANES,),
        in_specs=[pl.BlockSpec(weights.shape, lambda j: (0, 0))] + [lane(v) for v in (screened, *held)],
        out_specs=pl.BlockSpec((n_freq * height, LANES), lambda j: (0, j)),
        out_shape=shape((n_freq * height, width), f32),
        compiler_params=pltpu.CompilerParams(vmem_limit_bytes=28 * 2**20),
    )(weights, screened, *held)
    return sigma.reshape(n_freq, height, width)


def solution(mesh):
    devices = np.array(mesh.devices).reshape(4, 2, 2, 2, 4)
    fine = Mesh(devices, ("z", "xl", "c", "xh", "y"))
    tau, aux = ("z", "xl", "c"), ("xh", "y")
    return jax.shard_map(
        body,
        mesh=fine,
        in_specs=(P(tau, None, aux), P(), P(None, aux), P(), P(None, aux), P(tau, aux)),
        out_specs=P(None, tau, aux),
        check_vma=False,
    )
```

```python
import functools

import jax
import jax.numpy as jnp
import numpy as np
from jax import lax
from jax.experimental import pallas as pl
from jax.experimental.pallas import tpu as pltpu
from jax.sharding import Mesh, PartitionSpec as P

BLOCK = 128
LANES = 128
ANY = pl.BlockSpec(memory_space=pl.ANY)
WHOLE = pl.BlockSpec(memory_space=pltpu.VMEM)
SMALL = pltpu.CompilerParams(vmem_limit_bytes=14 * 2**20)
COST = pl.CostEstimate(flops=4 * 10**9, bytes_accessed=2 * 10**7, transcendentals=0)
LITTLE = pl.CostEstimate(flops=10**6, bytes_accessed=10**5, transcendentals=0)
LONG = pl.CostEstimate(flops=10**11, bytes_accessed=10**6, transcendentals=0)


def stage_kernel(source, after, held, sem):
    copy = pltpu.make_async_copy(source, held, sem)
    copy.start()
    copy.wait()


def join_kernel(a, b, c, d, out):
    for i, v in enumerate((a, b, c, d)):
        out[i] = v[...]


def fill(at, chunk, green_ref, mask_ref, rows_ref):
    times, _, height, cols = green_ref.shape
    base = lax.rem(at[2] + chunk, 4) * 4
    for i in range(4):
        marks = mask_ref[i ^ at[1]].astype(jnp.float32)
        for k in range(cols // BLOCK):
            keep = jnp.broadcast_to(marks[:, k : k + 1], (height, BLOCK)).astype(jnp.bfloat16)
            lanes = slice(k * BLOCK, (k + 1) * BLOCK)
            for t in range(times):
                row = (i * times + t) * height
                rows_ref[row : row + height, lanes] = green_ref[t, base + i, :, lanes] * keep


def product(rows_ref, a):
    return lax.dot_general(rows_ref[...], a, (((1,), (1,)), ((), ())), preferred_element_type=jnp.float32)


def put(out_ref, h, v):
    part = out_ref.shape[2]
    for i in range(4):
        out_ref[i, h] = v[i * part : (i + 1) * part].astype(out_ref.dtype)


def far_kernel(chunks, at, green_ref, aux_ref, after, *refs):
    mask_refs, (lo_ref, hi_ref, rows_ref) = refs[: len(chunks)], refs[-3:]
    target = lax.rem(at[0] + 2, aux_ref.shape[1])
    for q, chunk in enumerate(chunks):
        fill(at, chunk, green_ref, mask_refs[q], rows_ref)
        lo_ref[q] = product(rows_ref, aux_ref[0, target]).astype(jnp.bfloat16)
        hi_ref[q] = product(rows_ref, aux_ref[1, target]).astype(jnp.bfloat16)


def near_kernel(chunks, at, green_ref, aux_ref, after, *refs):
    rows_ref = refs[-1]
    n = aux_ref.shape[1]
    below, above = lax.rem(at[0] + n - 1, n), lax.rem(at[0] + 1, n)
    for q, chunk in enumerate(chunks):
        mask_ref, from_up, from_down = refs[3 * q : 3 * q + 3]
        down_ref, up_ref = refs[2 * q - 1 - 2 * len(chunks) :][:2]
        fill(at, chunk, green_ref, mask_ref, rows_ref)
        put(down_ref, 0, product(rows_ref, aux_ref[0, below]) + from_up[0].astype(jnp.float32))
        put(down_ref, 1, product(rows_ref, aux_ref[1, below]))
        put(up_ref, 0, product(rows_ref, aux_ref[0, above]))
        put(up_ref, 1, product(rows_ref, aux_ref[1, above]) + from_down[0].astype(jnp.float32))


def own_kernel(chunks, at, green_ref, aux_ref, after, *refs):
    n, rows_ref = len(chunks), refs[-1]
    for q, chunk in enumerate(chunks):
        fill(at, chunk, green_ref, refs[q], rows_ref)
        for h in range(2):
            put(refs[n + q], h, product(rows_ref, aux_ref[h, at[0]]))


def sum_kernel(n, *refs):
    out_ref = refs[-1]
    for q in range(n):
        own_ref, from_up, from_down = refs[3 * q : 3 * q + 3]
        for i in range(4):
            for h in range(2):
                others = from_up[i, h].astype(jnp.float32) + from_down[i, h].astype(jnp.float32)
                out_ref[2 * i + h, q] = (own_ref[i, h] + others).astype(out_ref.dtype)


def gather_kernel(got_ref, after, *out_refs):
    part = got_ref.shape[2]
    for q, out_ref in enumerate(out_refs):
        for i in range(4):
            both = got_ref[2 * i, q].astype(jnp.float32) + got_ref[2 * i + 1, q].astype(jnp.float32)
            out_ref[i * part : (i + 1) * part] = both


def final_kernel(w_ref, s_ref, *refs):
    x_refs, o_ref = refs[:-1], refs[-1]
    n_freq, _ = w_ref.shape
    height = o_ref.shape[0] // n_freq
    part = 8 * height
    w = w_ref[...]
    high = w.astype(jnp.bfloat16)
    low = (w - high.astype(jnp.float32)).astype(jnp.bfloat16)
    twice = jnp.concatenate([high, high], axis=1)
    scale = jnp.concatenate([s_ref[...], s_ref[...]], axis=0)

    def row(m):
        return jnp.concatenate(
            [ref[pl.ds(i * part + m, 8, stride=height), :] for ref in x_refs for i in range(ref.shape[0] // part)],
            axis=0,
        )

    for m in range(0, height, 2):
        x = jnp.concatenate([row(m), row(m + 1)], axis=1)
        x_high = x.astype(jnp.bfloat16)
        x_low = (x - x_high.astype(jnp.float32)).astype(jnp.bfloat16)
        mixed = jnp.dot(
            twice, jnp.concatenate([x_high, x_low], axis=0), preferred_element_type=jnp.float32
        ) + jnp.dot(low, x_high, preferred_element_type=jnp.float32)
        o_ref[pl.ds(m, n_freq, stride=height), :] = mixed[:, :LANES] * scale
        o_ref[pl.ds(m + 1, n_freq, stride=height), :] = mixed[:, LANES:] * scale


def body(green_tau, fit_matrix, aux_factors, freq_basis, screened, pair_mask):
    z, xl, c, y = (lax.axis_index(a) for a in ("z", "xl", "c", "y"))
    nz, ny = lax.axis_size("z"), lax.axis_size("y")
    times, n_rows, cols = green_tau.shape
    height, blocks = pair_mask.shape
    width = aux_factors.shape[0] // (2 * ny)
    part = times * height
    rows = 4 * part
    f32, bf16 = jnp.float32, jnp.bfloat16
    shape = jax.ShapeDtypeStruct

    def shift(v, axis, by):
        n = lax.axis_size(axis)
        return lax.ppermute(v, axis, [(i, (i + by) % n) for i in range(n)])

    exact = lax.Precision.HIGHEST
    order = jnp.stack([(z + nz - d) % nz for d in range(nz)])
    source = (order[:, None] * (4 * times) + jnp.arange(4 * times)[None, :]).reshape(1, -1)
    n_time = source.shape[1]
    pick = (jnp.arange(n_time)[:, None] == source).astype(f32)
    picked = jnp.dot(fit_matrix.astype(f32), pick, precision=exact)
    weights = jnp.dot(freq_basis, picked, precision=exact)
    at = jnp.stack([y, xl * 2 + c, z]).astype(jnp.int32)

    def stage(v, after):
        out = pl.pallas_call(
            stage_kernel,
            in_specs=[pl.BlockSpec(memory_space=pltpu.HBM), ANY],
            out_specs=WHOLE,
            out_shape=pltpu.VMEM(v.shape, v.dtype),
            scratch_shapes=[pltpu.SemaphoreType.DMA],
            compiler_params=SMALL,
            cost_estimate=COST,
        )(v, after)
        return pltpu.with_memory_space_constraint(out, pltpu.VMEM)

    def swap(v, e, f):
        pairs = [(i * 2 + j, (i ^ e) * 2 + (j ^ f)) for i in (0, 1) for j in (0, 1)]
        return lax.ppermute(v, ("xl", "c"), pairs)

    aux = stage(aux_factors.reshape(2, ny, width, cols), at)
    quad = pl.pallas_call(
        join_kernel,
        out_shape=shape((4, height, blocks), pair_mask.dtype),
        compiler_params=SMALL,
        cost_estimate=LITTLE,
    )(pair_mask, swap(pair_mask, 0, 1), swap(pair_mask, 1, 0), swap(pair_mask, 1, 1))
    marks = [quad if d == 0 else shift(quad, "z", -d) for d in range(nz)]
    green = stage(green_tau.reshape(times, n_rows // height, height, cols), quad)

    def call(kernel, after, extra, extra_specs, out_shape, cost=COST):
        fixed = lambda s: pl.BlockSpec(s.shape, lambda j, at: (0,) * len(s.shape))
        outs = out_shape if isinstance(out_shape, list) else [out_shape]
        got = pl.pallas_call(
            kernel,
            grid_spec=pltpu.PrefetchScalarGridSpec(
                num_scalar_prefetch=1,
                grid=(1,),
                in_specs=[WHOLE, WHOLE, ANY] + [s or fixed(v) for s, v in zip(extra_specs, extra, strict=True)],
                out_specs=[fixed(s) for s in outs],
                scratch_shapes=[pltpu.VMEM((rows, cols), bf16)],
            ),
            out_shape=outs,
            compiler_params=SMALL,
            cost_estimate=cost,
        )(at, green, aux, after, *extra)
        return got if isinstance(out_shape, list) else got[0]

    step1 = {}

    def far(chunks, after, arrived=()):
        out = shape((len(chunks), rows, width), bf16)
        lo, hi = call(
            functools.partial(far_kernel, chunks), after,
            [*(marks[d] for d in chunks), *arrived], [None] * len(chunks) + [ANY] * len(arrived), [out, out],
        )
        got = shift(lo, "y", -1), shift(hi, "y", 1)
        for q, d in enumerate(chunks):
            step1[d] = q, got
        return lo

    message = (4, 2, part, width)
    step2 = {}

    def near(chunks, after, arrived=(), cost=COST):
        args, specs = [], []
        for d in chunks:
            q, got = step1[d]
            spec = pl.BlockSpec((1, rows, width), lambda j, at, q=q: (q, 0, 0))
            args += [marks[d], *got]
            specs += [None, spec, spec]
        out = call(
            functools.partial(near_kernel, chunks), after, args + [*arrived], specs + [ANY] * len(arrived),
            [shape(message, bf16)] * (2 * len(chunks)), cost,
        )
        for k, d in enumerate(chunks):
            step2[d] = shift(out[2 * k], "y", -1), shift(out[2 * k + 1], "y", 1)
        return out[0]

    def own(after):
        chunks = tuple(range(nz))
        return call(
            functools.partial(own_kernel, chunks), after, [marks[d] for d in chunks], [None] * nz,
            [shape(message, f32)] * nz,
        )

    crossed = {}

    def cross(chunks, after, kind, cost=LITTLE):
        n = len(chunks)
        fixed = pl.BlockSpec(message, lambda j: (0, 0, 0, 0))
        total = pl.pallas_call(
            functools.partial(sum_kernel, n),
            grid=(1,),
            in_specs=[fixed] * (3 * n) + [ANY],
            out_specs=pl.BlockSpec((8, n, part, width), lambda j: (0, 0, 0, 0)),
            out_shape=shape((8, n, part, width), kind),
            compiler_params=SMALL,
            cost_estimate=cost,
        )(*[v for d in chunks for v in (mine[d], *step2[d])], after)
        crossed[chunks] = lax.all_to_all(total, ("xl", "c", "xh"), split_axis=0, concat_axis=0, tiled=True)
        return total

    pieces = {}

    def gather(chunks, after):
        got = crossed[chunks]
        outs = pl.pallas_call(
            gather_kernel,
            in_specs=[pl.BlockSpec(got.shape, lambda: (0, 0, 0, 0)), ANY],
            out_shape=[shape((rows, width), f32)] * len(chunks),
            compiler_params=SMALL,
            cost_estimate=LITTLE,
        )(got, after)
        for d, out in zip(chunks, outs, strict=True):
            pieces[d] = out if d == 0 else shift(out, "z", d)
        return outs[0]

    last = far((2, 0), quad, (marks[1], marks[3]))
    last = far((1, 3), last)
    mine = own(last)
    last = near((2,), mine[0])
    last = near((1,), last)
    last = near((3, 0), last, cost=LITTLE)
    last = cross((2,), last, f32)
    last = cross((1, 3), last, bf16, LONG)
    last = gather((2,), last)
    last = cross((0,), last, bf16, LONG)
    last = gather((1, 3), last)
    gather((0,), last)

    n_freq = weights.shape[0]
    lane = lambda v: pl.BlockSpec((v.shape[0], LANES), lambda j: (0, j))
    held = [pieces[d] for d in range(nz)]
    sigma = pl.pallas_call(
        final_kernel,
        grid=(width // LANES,),
        in_specs=[pl.BlockSpec(weights.shape, lambda j: (0, 0))] + [lane(v) for v in (screened, *held)],
        out_specs=pl.BlockSpec((n_freq * height, LANES), lambda j: (0, j)),
        out_shape=shape((n_freq * height, width), f32),
        compiler_params=pltpu.CompilerParams(vmem_limit_bytes=28 * 2**20),
    )(weights, screened, *held)
    return sigma.reshape(n_freq, height, width)


def solution(mesh):
    devices = np.array(mesh.devices).reshape(4, 2, 2, 2, 4)
    fine = Mesh(devices, ("z", "xl", "c", "xh", "y"))
    tau, aux = ("z", "xl", "c"), ("xh", "y")
    return jax.shard_map(
        body,
        mesh=fine,
        in_specs=(P(tau, None, aux), P(), P(None, aux), P(), P(None, aux), P(tau, aux)),
        out_specs=P(None, tau, aux),
        check_vma=False,
    )
```
